768 devices in a mesh: slab: 48 (over z, x), tile: 16 (over y, core).
Axes of the slice: x: 4, y: 8, z: 12, core: 2. Of those that a mesh axis runs over, the one named last changes fastest.
Arguments:
- tiles: bfloat16 [768, 20, 256, 128], P(('slab', 'tile')), may hold values from -6 to 6
- offsets: int32 [768, 2], replicated, may hold values from -3 to 3450, as said below
- fracs: int32 [768, 3], replicated, may hold values from 0 to 15
Outputs:
- joined: bfloat16 [768, 3706, 128], P(('slab', 'tile'))
The draws below stay inside these ranges and needn't reach their ends.
Inputs may be any that keep to these rules, and one draw needn't show every extreme that they name: offsets[g, 0] lies within 1 of (g // 16) * 16 - 2, and offsets[g, 1] within 4 of (g % 16) * 230, clipped to 0 .. 3450; some tile reaches each end of the plane shift.
All inputs are finite; a program needn't handle non-finite values.
Results may differ from the reference program's by a relative error of at most 0.0038.
Values may be sent and summed in bfloat16 or wider, within the bound.
No kernel may reach another device: no remote copies, remote signals or barrier semaphores. Data moves between devices by JAX's collectives and lax.ppermute only.
A program may use at most 32 MiB of HBM per device.

```python
import jax
import jax.numpy as jnp
from jax import lax

GROUPZ = 16
MARGIN = 2
JIT = 1
TY = 256
TX = 128
STEPY = 230
JITY = 4
RY = 26
RX = 16
QUANT = 16
TZ = 20
TILES_GROUP = 16
TILES = 768
MY = 3706
NZ = 768


def draw_offsets(key, part):
    key_plane = jax.random.fold_in(key, 11)
    key_row = jax.random.fold_in(key, 12)
    key_lowest = jax.random.fold_in(key, 13)
    key_highest = jax.random.fold_in(key, 14)
    position = jnp.arange(TILES, dtype=jnp.int32)
    group_of = position // TILES_GROUP
    within = position % TILES_GROUP
    shift_plane = jax.random.randint(key_plane, (TILES,), -JIT, JIT + 1)
    lowest_tile = jax.random.randint(key_lowest, (), 0, TILES)
    highest_tile = (lowest_tile + 1 + jax.random.randint(key_highest, (), 0, TILES - 1)) % TILES
    shift_plane = jnp.where(position == lowest_tile, -JIT, shift_plane)
    shift_plane = jnp.where(position == highest_tile, JIT, shift_plane)
    first_plane = group_of * GROUPZ - MARGIN + shift_plane
    shift_row = jax.random.randint(key_row, (TILES,), -JITY, JITY + 1)
    first_row = jnp.clip(within * STEPY + shift_row, 0, MY - TY)
    return jnp.stack([first_plane, first_row], axis=1).astype(jnp.int32)


def set_ends(drawn, key, low, largest):
    shape = drawn.shape
    index_at = [jax.random.randint(jax.random.fold_in(key, axis), (), 0, shape[axis]) for axis in range(len(shape))]
    drawn = drawn.at[tuple(index_at)].set(low)
    longest = shape.index(max(shape))
    index_at[longest] = (index_at[longest] + 1) % shape[longest]
    return drawn.at[tuple(index_at)].set(largest)


def levels(key, shape, pieces, least, top_value):
    def one(dim, shards_of):
        draws = jax.random.uniform(jax.random.fold_in(jax.random.fold_in(key, 6), dim), (shards_of,), jnp.float32, least / len(pieces), top_value / len(pieces))
        return jnp.repeat(jnp.exp(draws), shape[dim] // shards_of).reshape((-1,) + (1,) * (len(shape) - dim - 1))

    level = one(*pieces[0])
    for cut in pieces[1:]:
        level = level * one(*cut)
    return level


def centred(own_key, shape, scale, most, shards=(), held_as=jnp.bfloat16):
    entries = scale * jax.random.normal(own_key, shape, jnp.float32)
    if shards:
        entries = entries * levels(own_key, shape, shards, -0.22, 0.18)
    return jnp.clip(entries, -most, most).astype(held_as)


def setup_inputs(seed: int = 0) -> dict:
    splits = jax.random.split(jax.random.key(seed), 4)
    tiles = centred(splits[0], (TILES, TZ, TY, TX), 1.0, 6.0, ((0, 768),))
    offsets = draw_offsets(jax.random.fold_in(splits[3], 71), 0)
    fracs = set_ends(jax.random.randint(splits[2], (TILES, 3), 0, QUANT), jax.random.fold_in(splits[2], 1), 0, QUANT - 1).astype(jnp.int32)
    return {"tiles": tiles, "offsets": offsets, "fracs": fracs}


weight_floor = 0.05


def ramp(length, ramp_width):
    position = jnp.arange(length, dtype=jnp.float32)
    rising = 0.5 - 0.5 * jnp.cos(jnp.pi * (position + 1.0) / (ramp_width + 1.0))
    rising = jnp.where(position < ramp_width, rising, jnp.ones_like(rising))
    return jnp.minimum(rising, rising[::-1])


def resample(raw_tile, fraction_row):
    volume_field = raw_tile.astype(jnp.float32)
    for direction in range(3):
        fraction = fraction_row[direction].astype(jnp.float32) / QUANT
        extent = volume_field.shape[direction]
        shifted = jnp.concatenate([lax.slice_in_dim(volume_field, 1, extent, axis=direction), jnp.zeros_like(lax.slice_in_dim(volume_field, 0, 1, axis=direction))], axis=direction)
        volume_field = (1.0 - fraction) * volume_field + fraction * shifted
    return volume_field


def reference(tiles, offsets, fracs):
    ramp_z = ramp(TZ, 2 * MARGIN)
    ramp_y = ramp(TY, RY)
    ramp_x = ramp(TX, RX)
    weight = ramp_z[:, None, None] * ramp_y[None, :, None] * ramp_x[None, None, :]
    border = MARGIN + JIT
    numer_init = jnp.zeros((NZ + 2 * border, MY, TX), jnp.float32)
    weight_init = jnp.zeros((NZ + 2 * border, MY, TX), jnp.float32)

    def place(totals, element):
        numer, weight_sum = totals
        one_tile, corner, fraction_row = element
        blended = (resample(one_tile, fraction_row) * weight).astype(jnp.bfloat16)
        start_at = ((corner[0] + border).astype(jnp.int32), corner[1].astype(jnp.int32), jnp.zeros((), jnp.int32))
        current = lax.dynamic_slice(numer, start_at, (TZ, TY, TX))
        numer = lax.dynamic_update_slice(numer, current + blended.astype(jnp.float32), start_at)
        current = lax.dynamic_slice(weight_sum, start_at, (TZ, TY, TX))
        weight_sum = lax.dynamic_update_slice(weight_sum, current + weight, start_at)
        return (numer, weight_sum), None

    (numer, weight_sum), _ = lax.scan(place, (numer_init, weight_init), (tiles, offsets, fracs))
    numer = numer[border:border + NZ]
    weight_sum = weight_sum[border:border + NZ]
    return (numer / jnp.maximum(weight_sum, weight_floor)).astype(jnp.bfloat16)
```

```python
import functools

import jax
import jax.numpy as jnp
import numpy as np
from jax import lax
from jax.experimental import pallas as pl
from jax.experimental.pallas import tpu as pltpu
from jax.sharding import PartitionSpec as P

GROUPZ = 16
MARGIN = 2
JIT = 1
RIM = MARGIN + JIT
TY = 256
TX = 128
TZ = 20
STEPY = 230
JITY = 4
RY = 26
RX = 16
QUANT = 16
RANKS = 16
MY = 3706
FLOOR = 0.05

FRAME = 272
PAD = 16
SPAN = 16 + FRAME + 16
MYP = 3712

BASES = [max(0, (STEPY * r - JITY) // 8 * 8) for r in range(RANKS)]
LOW = tuple(range(RIM))
HIGH = tuple(range(GROUPZ - RIM, GROUPZ))

VMEM = pl.BlockSpec(memory_space=pltpu.VMEM)
SMEM = pl.BlockSpec(memory_space=pltpu.SMEM)
ANY = pl.BlockSpec(memory_space=pl.ANY)


def ramp(length, ramp_width):
    position = np.arange(length, dtype=np.float64)
    rising = 0.5 - 0.5 * np.cos(np.pi * (position + 1.0) / (ramp_width + 1.0))
    rising = np.where(position < ramp_width, rising, 1.0)
    return np.minimum(rising, rising[::-1]).astype(np.float32)


RAMP_Z = [float(v) for v in ramp(TZ, 2 * MARGIN)]


def row_table():
    table = np.zeros((SPAN, TX), np.float32)
    table[PAD : PAD + TY] = ramp(TY, RY)[:, None]
    return jnp.asarray(table)


def column_table():
    wx = ramp(TX, RX)
    cut = wx.copy()
    cut[-1] = 0.0
    table = np.zeros((8, TX), np.float32)
    table[0], table[1] = wx, cut
    return jnp.asarray(table)


def weight_z(plane):
    near = jnp.minimum(plane, TZ - 1 - plane)
    value = jnp.where(near < 0, jnp.float32(0.0), jnp.float32(1.0))
    for i in range(2 * MARGIN):
        value = jnp.where(near == i, jnp.float32(RAMP_Z[i]), value)
    return value


def base_of(rank):
    return jnp.maximum((STEPY * rank - JITY) // 8 * 8, 0)


def spot():
    return lax.axis_index("slab"), lax.axis_index("tile")


def fraction(fracs_ref, tile, direction):
    return fracs_ref[direction, tile].astype(jnp.float32) * (1.0 / QUANT)


def rims_kernel(tiles_ref, fracs_ref, low_ref, high_ref, held, sems):
    slab, rank = spot()
    tile = slab * RANKS + rank
    first = pltpu.make_async_copy(tiles_ref.at[0, pl.ds(0, RIM + 1)], held.at[pl.ds(0, RIM + 1)], sems.at[0])
    last = pltpu.make_async_copy(tiles_ref.at[0, pl.ds(TZ - RIM, RIM)], held.at[pl.ds(RIM + 1, RIM)], sems.at[1])
    first.start()
    last.start()
    f = fraction(fracs_ref, tile, 0)
    first.wait()
    for p in range(RIM):
        low_ref[p] = ((1.0 - f) * held[p].astype(jnp.float32) + f * held[p + 1].astype(jnp.float32)).astype(jnp.bfloat16)
    last.wait()
    for p in range(RIM):
        here = (1.0 - f) * held[RIM + 1 + p].astype(jnp.float32)
        if p < RIM - 1:
            here = here + f * held[RIM + 2 + p].astype(jnp.float32)
        high_ref[p] = here.astype(jnp.bfloat16)


def row_terms(table_ref, terms, shift, f):
    w = table_ref[pl.ds(PAD - shift, FRAME), :]
    terms[0] = (1.0 - f) * w
    terms[1] = f * w


def blend(held, slot, terms, shift, c0, c1):
    u = held[slot, pl.ds(PAD - shift, FRAME), :] * terms[0] + held[slot, pl.ds(PAD + 1 - shift, FRAME), :] * terms[1]
    return u * c0 + pltpu.roll(u, TX - 1, 1) * c1


def own_kernel(tiles_ref, offsets_ref, fracs_ref, table_ref, cols_ref, out_ref, rim_ref, held, terms, sent, sems):
    slab, rank = spot()
    tile = slab * RANKS + rank
    shift = offsets_ref[1, tile] - base_of(rank)
    first = slab * GROUPZ - offsets_ref[0, tile]
    fz, fy, fx = [fraction(fracs_ref, tile, d) for d in range(3)]
    row_terms(table_ref, terms, shift, fy)
    c0 = (1.0 - fx) * cols_ref[0:1, :]
    c1 = fx * cols_ref[1:2, :]
    for slot in range(2):
        held[slot, 0:PAD, :] = jnp.zeros((PAD, TX), jnp.float32)
        held[slot, PAD + TY : SPAN, :] = jnp.zeros((SPAN - PAD - TY, TX), jnp.float32)

    def plane(z, slot):
        p = first + z
        w = weight_z(p)
        held[slot, PAD : PAD + TY, :] = (w * (1.0 - fz)) * tiles_ref[0, p].astype(jnp.float32) + (w * fz) * tiles_ref[
            0, p + 1
        ].astype(jnp.float32)
        return blend(held, slot, terms, shift, c0, c1)

    for i, z in enumerate(LOW + HIGH):
        rim_ref[i] = plane(z, i % 2)
    copies = []
    for i in range(GROUPZ - 2 * RIM):
        sent[i] = plane(RIM + i, i % 2).astype(jnp.bfloat16)
        copies.append(pltpu.make_async_copy(sent.at[i], out_ref.at[RIM + i], sems.at[i]))
        copies[-1].start()
    for copy in copies:
        copy.wait()


def merge_kernel(frames_ref, rim_ref, below_ref, above_ref, offsets_ref, fracs_ref, table_ref, cols_ref, out_ref, held, terms, sent, sems):
    slab, rank = spot()
    last = lax.axis_size("slab") - 1
    for slot in range(2):
        held[slot, 0:PAD, :] = jnp.zeros((PAD, TX), jnp.float32)
        held[slot, PAD + TY : SPAN, :] = jnp.zeros((SPAN - PAD - TY, TX), jnp.float32)
    for side, (planes, source_ref) in enumerate(((LOW, below_ref), (HIGH, above_ref))):
        group = slab - 1 if side == 0 else slab + 1
        valid = jnp.logical_and(group >= 0, group <= last)
        tile = jnp.clip(group, 0, last) * RANKS + rank
        shift = offsets_ref[1, tile] - base_of(rank)
        first = slab * GROUPZ - offsets_ref[0, tile]
        first = jnp.where(valid, first, 2 * TZ)
        row_terms(table_ref, terms, shift, fraction(fracs_ref, tile, 1))
        fx = fraction(fracs_ref, tile, 2)
        c0 = (1.0 - fx) * cols_ref[0:1, :]
        c1 = fx * cols_ref[1:2, :]
        for i, z in enumerate(planes):
            p = first + z
            w = weight_z(p)
            at = jnp.clip(p - (TZ - RIM) if side == 0 else p, 0, RIM - 1)
            held[i % 2, PAD : PAD + TY, :] = w * source_ref[at].astype(jnp.float32)
            total = rim_ref[side * RIM + i] + blend(held, i % 2, terms, shift, c0, c1)
            sent[side * RIM + i] = total.astype(jnp.bfloat16)
    copies = []
    for side, planes in enumerate((LOW, HIGH)):
        copies.append(
            pltpu.make_async_copy(sent.at[pl.ds(side * RIM, RIM)], out_ref.at[pl.ds(planes[0], RIM)], sems.at[side])
        )
        copies[-1].start()
    for copy in copies:
        copy.wait()


def weights_kernel(offsets_ref, table_ref, cols_ref, out_ref):
    slab, rank = spot()
    last = lax.axis_size("slab") - 1
    z = slab * GROUPZ + rank
    side = jnp.where(rank < RANKS // 2, slab - 1, slab + 1)
    valid = jnp.logical_and(side >= 0, side <= last)
    out_ref[...] = jnp.zeros_like(out_ref)
    for r in range(RANKS):
        total = 0.0
        for group, usable in ((slab, None), (jnp.clip(side, 0, last), valid)):
            tile = group * RANKS + r
            w = weight_z(z - offsets_ref[0, tile])
            if usable is not None:
                w = jnp.where(usable, w, 0.0)
            total = total + w * table_ref[pl.ds(PAD + BASES[r] - offsets_ref[1, tile], FRAME), :]
        out_ref[BASES[r] : BASES[r] + FRAME, :] += total
    out_ref[...] = 1.0 / jnp.maximum(out_ref[...] * cols_ref[0:1, :], FLOOR)


def join_kernel(frames_ref, recip_ref, out_ref, held):
    done = 0
    for r in range(RANKS):
        base = BASES[r]
        for k in range(0, FRAME, 16):
            piece = frames_ref[r, k : k + 16, :].astype(jnp.float32)
            for h in (0, 8):
                row = base + k + h
                part = piece[h : h + 8]
                if row < done:
                    held[row : row + 8, :] += part
                else:
                    held[row : row + 8, :] = part
        done = base + FRAME
    for k in range(0, MY, 16):
        n = min(16, MY - k)
        out_ref[0, k : k + n, :] = (held[k : k + n, :] * recip_ref[k : k + n, :]).astype(jnp.bfloat16)


def cost(flops, moved):
    return pl.CostEstimate(flops=flops, bytes_accessed=moved, transcendentals=0)


def beside(block, distance):
    devices = range(lax.axis_size("slab"))
    return lax.ppermute(block, "slab", [(i, i + distance) for i in devices if i + distance in devices])


def shards(tiles, offsets, fracs):
    call = functools.partial(pl.pallas_call)
    params = pltpu.CompilerParams(vmem_limit_bytes=32 * 2**20)
    shape = jax.ShapeDtypeStruct
    offsets, fracs = offsets.T, fracs.T
    rows, cols = row_table(), column_table()
    rim = shape((RIM, TY, TX), jnp.bfloat16)
    work = [pltpu.VMEM((2, SPAN, TX), jnp.float32), pltpu.VMEM((2, FRAME, TX), jnp.float32)]
    frames = shape((RANKS, FRAME, TX), jnp.bfloat16)

    low, high = call(
        rims_kernel,
        out_shape=(rim, rim),
        in_specs=[ANY, SMEM],
        out_specs=(VMEM, VMEM),
        scratch_shapes=[pltpu.VMEM((2 * RIM + 1, TY, TX), jnp.bfloat16), pltpu.SemaphoreType.DMA((2,))],
        compiler_params=params,
        cost_estimate=cost(10**6, 10**6),
        name="rims",
    )(tiles, fracs)
    above = beside(low, -1)
    below = beside(high, 1)
    own, own_rim = call(
        own_kernel,
        out_shape=(frames, shape((2 * RIM, FRAME, TX), jnp.float32)),
        in_specs=[VMEM, SMEM, SMEM, VMEM, VMEM],
        out_specs=(ANY, VMEM),
        scratch_shapes=[*work, pltpu.VMEM((GROUPZ - 2 * RIM, FRAME, TX), jnp.bfloat16), pltpu.SemaphoreType.DMA((GROUPZ - 2 * RIM,))],
        compiler_params=params,
        cost_estimate=cost(10**7, 3 * 10**6),
        name="own",
    )(tiles, offsets, fracs, rows, cols)
    merged = call(
        merge_kernel,
        out_shape=frames,
        in_specs=[ANY, VMEM, VMEM, VMEM, SMEM, SMEM, VMEM, VMEM],
        out_specs=ANY,
        scratch_shapes=[*work, pltpu.VMEM((2 * RIM, FRAME, TX), jnp.bfloat16), pltpu.SemaphoreType.DMA((2,))],
        input_output_aliases={0: 0},
        compiler_params=params,
        cost_estimate=cost(3 * 10**6, 2 * 10**6),
        name="merge",
    )(own, own_rim, below, above, offsets, fracs, rows, cols)
    received = lax.all_to_all(merged, "tile", split_axis=0, concat_axis=0, tiled=True)
    recip = call(
        weights_kernel,
        out_shape=shape((MYP, TX), jnp.float32),
        in_specs=[SMEM, VMEM, VMEM],
        out_specs=VMEM,
        compiler_params=params,
        cost_estimate=cost(10**7, 4 * 10**6),
        name="weights",
    )(offsets, rows, cols)
    return call(
        join_kernel,
        out_shape=shape((1, MY, TX), jnp.bfloat16),
        in_specs=[VMEM, VMEM],
        out_specs=VMEM,
        scratch_shapes=[pltpu.VMEM((MYP, TX), jnp.float32)],
        compiler_params=params,
        cost_estimate=cost(10**6, 4 * 10**6),
        name="join",
    )(received, recip)


def solution(mesh):
    in_specs = (P(("slab", "tile"), None, None, None), P(), P())
    out_specs = P(("slab", "tile"), None, None)
    return jax.shard_map(shards, mesh=mesh, in_specs=in_specs, out_specs=out_specs, check_vma=False)
```

```python
import functools

import jax
import jax.numpy as jnp
import numpy as np
from jax import lax
from jax.experimental import pallas as pl
from jax.experimental.pallas import tpu as pltpu
from jax.sharding import PartitionSpec as P

GROUPZ = 16
MARGIN = 2
JIT = 1
RIM = MARGIN + JIT
TY = 256
TX = 128
TZ = 20
STEPY = 230
JITY = 4
RY = 26
RX = 16
QUANT = 16
RANKS = 16
MY = 3706
FLOOR = 0.05

FRAME = TY + 2 * JITY
STRIP = 272
PAD = 16
SPAN = 16 + STRIP + 16
MYP = 3712

BASES = [max(0, STEPY * r - JITY) for r in range(RANKS)]
LOW = tuple(range(RIM))
HIGH = tuple(range(GROUPZ - RIM, GROUPZ))

VMEM = pl.BlockSpec(memory_space=pltpu.VMEM)
SMEM = pl.BlockSpec(memory_space=pltpu.SMEM)
ANY = pl.BlockSpec(memory_space=pl.ANY)
HBM = pl.BlockSpec(memory_space=pltpu.HBM)


def ramp(length, ramp_width):
    position = np.arange(length, dtype=np.float64)
    rising = 0.5 - 0.5 * np.cos(np.pi * (position + 1.0) / (ramp_width + 1.0))
    rising = np.where(position < ramp_width, rising, 1.0)
    return np.minimum(rising, rising[::-1]).astype(np.float32)


RAMP_Z = [float(v) for v in ramp(TZ, 2 * MARGIN)]


def row_table():
    table = np.zeros((SPAN, TX), np.float32)
    table[PAD : PAD + TY] = ramp(TY, RY)[:, None]
    return jnp.asarray(table)


def column_table():
    wx = ramp(TX, RX)
    cut = wx.copy()
    cut[-1] = 0.0
    table = np.zeros((8, TX), np.float32)
    table[0], table[1] = wx, cut
    return jnp.asarray(table)


def weight_z(plane):
    near = jnp.minimum(plane, TZ - 1 - plane)
    value = jnp.where(near < 0, jnp.float32(0.0), jnp.float32(1.0))
    for i in range(2 * MARGIN):
        value = jnp.where(near == i, jnp.float32(RAMP_Z[i]), value)
    return value


def base_of(rank):
    return jnp.maximum(STEPY * rank - JITY, 0)


def spot():
    return lax.axis_index("slab"), lax.axis_index("tile")


def fraction(fracs_ref, tile, direction):
    return fracs_ref[direction, tile].astype(jnp.float32) * (1.0 / QUANT)


def row_terms(table_ref, terms, shift, f):
    w = table_ref[pl.ds(PAD - shift, FRAME), :]
    terms[0] = (1.0 - f) * w
    terms[1] = f * w


def blend(held, slot, terms, shift, c0, c1):
    u = held[slot, pl.ds(PAD - shift, FRAME), :] * terms[0] + held[slot, pl.ds(PAD + 1 - shift, FRAME), :] * terms[1]
    return u * c0 + pltpu.roll(u, TX - 1, 1) * c1


def clear_edges(held):
    for slot in range(2):
        held[slot, 0:PAD, :] = jnp.zeros((PAD, TX), jnp.float32)
        held[slot, PAD + TY : SPAN, :] = jnp.zeros((SPAN - PAD - TY, TX), jnp.float32)


def tile_terms(offsets_ref, fracs_ref, table_ref, cols_ref, terms):
    slab, rank = spot()
    tile = slab * RANKS + rank
    shift = offsets_ref[1, tile] - base_of(rank)
    fz, fy, fx = [fraction(fracs_ref, tile, d) for d in range(3)]
    row_terms(table_ref, terms, shift, fy)
    return offsets_ref[0, tile], shift, fz, (1.0 - fx) * cols_ref[0:1, :], fx * cols_ref[1:2, :]


def rims_kernel(tiles_ref, offsets_hbm, fracs_hbm, table_hbm, cols_hbm, one_ref, two_ref, planes, offsets_ref, fracs_ref, table_ref, cols_ref, held, terms, sems):
    copies = [
        pltpu.make_async_copy(offsets_hbm, offsets_ref, sems.at[0]),
        pltpu.make_async_copy(fracs_hbm, fracs_ref, sems.at[1]),
        pltpu.make_async_copy(table_hbm, table_ref, sems.at[2]),
        pltpu.make_async_copy(cols_hbm, cols_ref, sems.at[3]),
        pltpu.make_async_copy(tiles_ref.at[0, pl.ds(0, RIM + 1)], planes.at[pl.ds(0, RIM + 1)], sems.at[4]),
        pltpu.make_async_copy(tiles_ref.at[0, pl.ds(TZ - RIM, RIM)], planes.at[pl.ds(RIM + 1, RIM)], sems.at[5]),
    ]
    for copy in copies:
        copy.start()
    clear_edges(held)
    for copy in copies:
        copy.wait()
    slab, _ = spot()
    origin, shift, fz, c0, c1 = tile_terms(offsets_ref, fracs_ref, table_ref, cols_ref, terms)
    for turn, out_ref in enumerate((one_ref, two_ref)):
        upward = slab % 2 != turn
        first = jnp.where(upward, (slab + 1) * GROUPZ, slab * GROUPZ - RIM) - origin
        skipped = jnp.where(upward, TZ - RIM - (RIM + 1), 0)
        for i in range(RIM):
            p = first + i
            w = weight_z(p)
            after = jnp.where(p < TZ - 1, w * fz, 0.0)
            here = jnp.clip(p - skipped, 0, 2 * RIM)
            there = jnp.clip(p + 1 - skipped, 0, 2 * RIM)
            held[i % 2, PAD : PAD + TY, :] = (w * (1.0 - fz)) * planes[here].astype(jnp.float32) + after * planes[
                there
            ].astype(jnp.float32)
            out_ref[i] = blend(held, i % 2, terms, shift, c0, c1).astype(jnp.bfloat16)


def own_kernel(tiles_ref, offsets_ref, fracs_ref, table_ref, cols_ref, out_ref, rim_ref, held, terms, sent, sems):
    slab, _ = spot()
    origin, shift, fz, c0, c1 = tile_terms(offsets_ref, fracs_ref, table_ref, cols_ref, terms)
    first = slab * GROUPZ - origin
    clear_edges(held)

    def plane(z, slot):
        p = first + z
        w = weight_z(p)
        held[slot, PAD : PAD + TY, :] = (w * (1.0 - fz)) * tiles_ref[0, p].astype(jnp.float32) + (w * fz) * tiles_ref[
            0, p + 1
        ].astype(jnp.float32)
        return blend(held, slot, terms, shift, c0, c1)

    copies = []
    for i in range(GROUPZ - 2 * RIM):
        sent[i] = plane(RIM + i, i % 2).astype(jnp.bfloat16)
        copies.append(pltpu.make_async_copy(sent.at[i], out_ref.at[RIM + i], sems.at[i]))
        copies[-1].start()
    for i, z in enumerate(LOW + HIGH):
        rim_ref[i] = plane(z, i % 2)
    for copy in copies:
        copy.wait()


def merge_kernel(frames_ref, rim_ref, one_ref, two_ref, out_ref, sent, sems):
    slab, _ = spot()
    copies = []
    for turn, source_ref in enumerate((one_ref, two_ref)):
        side = jnp.where(slab % 2 != turn, 1, 0)
        for i in range(RIM):
            sent[turn * RIM + i] = (rim_ref[side * RIM + i] + source_ref[i].astype(jnp.float32)).astype(jnp.bfloat16)
        copies.append(
            pltpu.make_async_copy(
                sent.at[pl.ds(turn * RIM, RIM)], out_ref.at[pl.ds(side * (GROUPZ - RIM), RIM)], sems.at[turn]
            )
        )
        copies[-1].start()
    for copy in copies:
        copy.wait()


def weights_kernel(offsets_ref, table_ref, cols_ref, out_ref):
    slab, rank = spot()
    last = lax.axis_size("slab") - 1
    z = slab * GROUPZ + rank
    side = jnp.where(rank < RANKS // 2, slab - 1, slab + 1)
    valid = jnp.logical_and(side >= 0, side <= last)
    out_ref[...] = jnp.zeros_like(out_ref)
    for r in range(RANKS):
        total = 0.0
        base = BASES[r] // 8 * 8
        for group, usable in ((slab, None), (jnp.clip(side, 0, last), valid)):
            tile = group * RANKS + r
            w = weight_z(z - offsets_ref[0, tile])
            if usable is not None:
                w = jnp.where(usable, w, 0.0)
            total = total + w * table_ref[pl.ds(PAD + base - offsets_ref[1, tile], STRIP), :]
        out_ref[base : base + STRIP, :] += total
    out_ref[...] = 1.0 / jnp.maximum(out_ref[...] * cols_ref[0:1, :], FLOOR)


def join_kernel(frames_ref, recip_ref, out_ref, held):
    done = 0
    for r in range(RANKS):
        base = BASES[r]
        for k in range(0, FRAME, 16):
            n = min(16, FRAME - k)
            part = frames_ref[r, k : k + n, :].astype(jnp.float32)
            row = base + k
            old = max(0, min(n, done - row))
            if old:
                held[row : row + old, :] += part[:old]
            if old < n:
                held[row + old : row + n, :] = part[old:]
        done = base + FRAME
    for k in range(0, MY, 16):
        n = min(16, MY - k)
        out_ref[0, k : k + n, :] = (held[k : k + n, :] * recip_ref[k : k + n, :]).astype(jnp.bfloat16)


def cost(flops, moved):
    return pl.CostEstimate(flops=flops, bytes_accessed=moved, transcendentals=0)


def exchange(block, turn):
    slabs = lax.axis_size("slab")
    pairs = [(i, i + 1) for i in range(1 - turn, slabs - 1, 2)]
    return lax.ppermute(block, "slab", pairs + [(b, a) for a, b in pairs])


def shards(tiles, offsets, fracs):
    call = functools.partial(pl.pallas_call)
    params = pltpu.CompilerParams(vmem_limit_bytes=32 * 2**20)
    wide = pltpu.CompilerParams(vmem_limit_bytes=60 * 2**20)
    shape = jax.ShapeDtypeStruct
    offsets, fracs = offsets.T, fracs.T
    rows, cols = row_table(), column_table()
    rim = shape((RIM, FRAME, TX), jnp.bfloat16)
    work = [pltpu.VMEM((2, SPAN, TX), jnp.float32), pltpu.VMEM((2, FRAME, TX), jnp.float32)]
    frames = shape((RANKS, FRAME, TX), jnp.bfloat16)

    one, two = call(
        rims_kernel,
        out_shape=(rim, rim),
        in_specs=[HBM] * 5,
        out_specs=(VMEM, VMEM),
        scratch_shapes=[
            pltpu.VMEM((2 * RIM + 1, TY, TX), jnp.bfloat16),
            pltpu.SMEM(offsets.shape, jnp.int32),
            pltpu.SMEM(fracs.shape, jnp.int32),
            pltpu.VMEM(rows.shape, jnp.float32),
            pltpu.VMEM(cols.shape, jnp.float32),
            *work,
            pltpu.SemaphoreType.DMA((6,)),
        ],
        compiler_params=wide,
        cost_estimate=cost(10**6, 10**6),
        name="rims",
    )(tiles, offsets, fracs, rows, cols)
    got_one, got_two = exchange(one, 0), exchange(two, 1)
    own, own_rim = call(
        own_kernel,
        out_shape=(frames, shape((2 * RIM, FRAME, TX), jnp.float32)),
        in_specs=[VMEM, SMEM, SMEM, VMEM, VMEM],
        out_specs=(ANY, VMEM),
        scratch_shapes=[
            *work,
            pltpu.VMEM((GROUPZ - 2 * RIM, FRAME, TX), jnp.bfloat16),
            pltpu.SemaphoreType.DMA((GROUPZ - 2 * RIM,)),
        ],
        compiler_params=params,
        cost_estimate=cost(10**7, 3 * 10**6),
        name="own",
    )(tiles, offsets, fracs, rows, cols)
    merged = call(
        merge_kernel,
        out_shape=frames,
        in_specs=[ANY, VMEM, VMEM, VMEM],
        out_specs=ANY,
        scratch_shapes=[pltpu.VMEM((2 * RIM, FRAME, TX), jnp.bfloat16), pltpu.SemaphoreType.DMA((2,))],
        input_output_aliases={0: 0},
        compiler_params=params,
        cost_estimate=cost(3 * 10**6, 2 * 10**6),
        name="merge",
    )(own, own_rim, got_one, got_two)
    received = lax.all_to_all(merged, "tile", split_axis=0, concat_axis=0, tiled=True)
    recip = call(
        weights_kernel,
        out_shape=shape((MYP, TX), jnp.float32),
        in_specs=[SMEM, VMEM, VMEM],
        out_specs=VMEM,
        compiler_params=params,
        cost_estimate=cost(10**7, 4 * 10**6),
        name="weights",
    )(offsets, rows, cols)
    return call(
        join_kernel,
        out_shape=shape((1, MY, TX), jnp.bfloat16),
        in_specs=[VMEM, VMEM],
        out_specs=VMEM,
        scratch_shapes=[pltpu.VMEM((MYP, TX), jnp.float32)],
        compiler_params=params,
        cost_estimate=cost(10**6, 4 * 10**6),
        name="join",
    )(received, recip)


def solution(mesh):
    in_specs = (P(("slab", "tile"), None, None, None), P(), P())
    out_specs = P(("slab", "tile"), None, None)
    return jax.shard_map(shards, mesh=mesh, in_specs=in_specs, out_specs=out_specs, check_vma=False)
```

```python
import functools

import jax
import jax.numpy as jnp
import numpy as np
from jax import lax
from jax.experimental import pallas as pl
from jax.experimental.pallas import tpu as pltpu
from jax.sharding import PartitionSpec as P

GROUPZ = 16
MARGIN = 2
JIT = 1
RIM = MARGIN + JIT
TY = 256
TX = 128
TZ = 20
STEPY = 230
JITY = 4
RY = 26
RX = 16
QUANT = 16
RANKS = 16
MY = 3706
FLOOR = 0.05

FRAME = TY + 2 * JITY
STRIP = 272
PAD = 16
SPAN = 16 + STRIP + 16
MYP = 3712

BASES = [max(0, STEPY * r - JITY) for r in range(RANKS)]
LOW = tuple(range(RIM))
HIGH = tuple(range(GROUPZ - RIM, GROUPZ))

VMEM = pl.BlockSpec(memory_space=pltpu.VMEM)
SMEM = pl.BlockSpec(memory_space=pltpu.SMEM)
ANY = pl.BlockSpec(memory_space=pl.ANY)
HBM = pl.BlockSpec(memory_space=pltpu.HBM)


def ramp(length, ramp_width):
    position = np.arange(length, dtype=np.float64)
    rising = 0.5 - 0.5 * np.cos(np.pi * (position + 1.0) / (ramp_width + 1.0))
    rising = np.where(position < ramp_width, rising, 1.0)
    return np.minimum(rising, rising[::-1]).astype(np.float32)


RAMP_Z = [float(v) for v in ramp(TZ, 2 * MARGIN)]


def row_table():
    table = np.zeros((SPAN, TX), np.float32)
    table[PAD : PAD + TY] = ramp(TY, RY)[:, None]
    return jnp.asarray(table)


def column_table():
    wx = ramp(TX, RX)
    cut = wx.copy()
    cut[-1] = 0.0
    table = np.zeros((8, TX), np.float32)
    table[0], table[1] = wx, cut
    return jnp.asarray(table)


def weight_z(plane):
    near = jnp.minimum(plane, TZ - 1 - plane)
    value = jnp.where(near < 0, jnp.float32(0.0), jnp.float32(1.0))
    for i in range(2 * MARGIN):
        value = jnp.where(near == i, jnp.float32(RAMP_Z[i]), value)
    return value


def base_of(rank):
    return jnp.maximum(STEPY * rank - JITY, 0)


def spot():
    return lax.axis_index("slab"), lax.axis_index("tile")


def fraction(fracs_ref, tile, direction):
    return fracs_ref[direction, tile].astype(jnp.float32) * (1.0 / QUANT)


def row_terms(table_ref, terms, shift, f):
    w = table_ref[pl.ds(PAD - shift, FRAME), :]
    terms[0] = (1.0 - f) * w
    terms[1] = f * w


def blend(held, slot, terms, shift, c0, c1):
    u = held[slot, pl.ds(PAD - shift, FRAME), :] * terms[0] + held[slot, pl.ds(PAD + 1 - shift, FRAME), :] * terms[1]
    return u * c0 + pltpu.roll(u, TX - 1, 1) * c1


def clear_edges(held):
    for slot in range(2):
        held[slot, 0:PAD, :] = jnp.zeros((PAD, TX), jnp.float32)
        held[slot, PAD + TY : SPAN, :] = jnp.zeros((SPAN - PAD - TY, TX), jnp.float32)


def tile_terms(offsets_ref, fracs_ref, table_ref, cols_ref, terms):
    slab, rank = spot()
    tile = slab * RANKS + rank
    shift = offsets_ref[1, tile] - base_of(rank)
    fz, fy, fx = [fraction(fracs_ref, tile, d) for d in range(3)]
    row_terms(table_ref, terms, shift, fy)
    return offsets_ref[0, tile], shift, fz, (1.0 - fx) * cols_ref[0:1, :], fx * cols_ref[1:2, :]


def rims_kernel(tiles_ref, offsets_hbm, fracs_hbm, table_hbm, cols_hbm, one_ref, two_ref, planes, offsets_ref, fracs_ref, table_ref, cols_ref, held, terms, sems):
    copies = [
        pltpu.make_async_copy(offsets_hbm, offsets_ref, sems.at[0]),
        pltpu.make_async_copy(fracs_hbm, fracs_ref, sems.at[1]),
        pltpu.make_async_copy(table_hbm, table_ref, sems.at[2]),
        pltpu.make_async_copy(cols_hbm, cols_ref, sems.at[3]),
        pltpu.make_async_copy(tiles_ref.at[0, pl.ds(0, RIM + 1)], planes.at[pl.ds(0, RIM + 1)], sems.at[4]),
        pltpu.make_async_copy(tiles_ref.at[0, pl.ds(TZ - RIM, RIM)], planes.at[pl.ds(RIM + 1, RIM)], sems.at[5]),
    ]
    for copy in copies:
        copy.start()
    clear_edges(held)
    for copy in copies:
        copy.wait()
    slab, rank = spot()
    origin, shift, fz, c0, c1 = tile_terms(offsets_ref, fracs_ref, table_ref, cols_ref, terms)
    for turn, out_ref in enumerate((one_ref, two_ref)):
        upward = (slab + rank) % 2 != turn
        first = jnp.where(upward, (slab + 1) * GROUPZ, slab * GROUPZ - RIM) - origin
        skipped = jnp.where(upward, TZ - RIM - (RIM + 1), 0)
        for i in range(RIM):
            p = first + i
            w = weight_z(p)
            after = jnp.where(p < TZ - 1, w * fz, 0.0)
            here = jnp.clip(p - skipped, 0, 2 * RIM)
            there = jnp.clip(p + 1 - skipped, 0, 2 * RIM)
            held[i % 2, PAD : PAD + TY, :] = (w * (1.0 - fz)) * planes[here].astype(jnp.float32) + after * planes[
                there
            ].astype(jnp.float32)
            out_ref[i] = blend(held, i % 2, terms, shift, c0, c1).astype(jnp.bfloat16)


def own_kernel(tiles_ref, offsets_ref, fracs_ref, table_ref, cols_ref, out_ref, rim_ref, held, terms, sent, sems):
    slab, _ = spot()
    origin, shift, fz, c0, c1 = tile_terms(offsets_ref, fracs_ref, table_ref, cols_ref, terms)
    first = slab * GROUPZ - origin
    clear_edges(held)

    def plane(z, slot):
        p = first + z
        w = weight_z(p)
        held[slot, PAD : PAD + TY, :] = (w * (1.0 - fz)) * tiles_ref[0, p].astype(jnp.float32) + (w * fz) * tiles_ref[
            0, p + 1
        ].astype(jnp.float32)
        return blend(held, slot, terms, shift, c0, c1)

    copies = []
    for i in range(GROUPZ - 2 * RIM):
        sent[i] = plane(RIM + i, i % 2).astype(jnp.bfloat16)
        copies.append(pltpu.make_async_copy(sent.at[i], out_ref.at[RIM + i], sems.at[i]))
        copies[-1].start()
    for i, z in enumerate(LOW + HIGH):
        rim_ref[i] = plane(z, i % 2)
    for copy in copies:
        copy.wait()


def merge_kernel(frames_ref, rim_ref, one_ref, two_ref, out_ref, sent, sems):
    slab, rank = spot()
    copies = []
    for turn, source_ref in enumerate((one_ref, two_ref)):
        side = jnp.where((slab + rank) % 2 != turn, 1, 0)
        for i in range(RIM):
            sent[turn * RIM + i] = (rim_ref[side * RIM + i] + source_ref[i].astype(jnp.float32)).astype(jnp.bfloat16)
        copies.append(
            pltpu.make_async_copy(
                sent.at[pl.ds(turn * RIM, RIM)], out_ref.at[pl.ds(side * (GROUPZ - RIM), RIM)], sems.at[turn]
            )
        )
        copies[-1].start()
    for copy in copies:
        copy.wait()


def weights_kernel(offsets_ref, table_ref, cols_ref, out_ref):
    slab, rank = spot()
    last = lax.axis_size("slab") - 1
    z = slab * GROUPZ + rank
    side = jnp.where(rank < RANKS // 2, slab - 1, slab + 1)
    valid = jnp.logical_and(side >= 0, side <= last)
    out_ref[...] = jnp.zeros_like(out_ref)
    for r in range(RANKS):
        total = 0.0
        base = BASES[r] // 8 * 8
        for group, usable in ((slab, None), (jnp.clip(side, 0, last), valid)):
            tile = group * RANKS + r
            w = weight_z(z - offsets_ref[0, tile])
            if usable is not None:
                w = jnp.where(usable, w, 0.0)
            total = total + w * table_ref[pl.ds(PAD + base - offsets_ref[1, tile], STRIP), :]
        out_ref[base : base + STRIP, :] += total
    out_ref[...] = 1.0 / jnp.maximum(out_ref[...] * cols_ref[0:1, :], FLOOR)


def join_kernel(frames_ref, recip_ref, out_ref, held):
    done = 0
    for r in range(RANKS):
        base = BASES[r]
        for k in range(0, FRAME, 16):
            n = min(16, FRAME - k)
            part = frames_ref[r, k : k + n, :].astype(jnp.float32)
            row = base + k
            old = max(0, min(n, done - row))
            if old:
                held[row : row + old, :] += part[:old]
            if old < n:
                held[row + old : row + n, :] = part[old:]
        done = base + FRAME
    for k in range(0, MY, 16):
        n = min(16, MY - k)
        out_ref[0, k : k + n, :] = (held[k : k + n, :] * recip_ref[k : k + n, :]).astype(jnp.bfloat16)


def cost(flops, moved):
    return pl.CostEstimate(flops=flops, bytes_accessed=moved, transcendentals=0)


def exchange(block, turn):
    slabs, ranks = lax.axis_size("slab"), lax.axis_size("tile")
    pairs = [(s * ranks + r, (s + 1) * ranks + r) for s in range(slabs - 1) for r in range(ranks) if (s + r) % 2 != turn]
    return lax.ppermute(block, ("slab", "tile"), pairs + [(b, a) for a, b in pairs])


def shards(tiles, offsets, fracs):
    call = functools.partial(pl.pallas_call)
    params = pltpu.CompilerParams(vmem_limit_bytes=32 * 2**20)
    wide = pltpu.CompilerParams(vmem_limit_bytes=60 * 2**20)
    shape = jax.ShapeDtypeStruct
    offsets, fracs = offsets.T, fracs.T
    rows, cols = row_table(), column_table()
    rim = shape((RIM, FRAME, TX), jnp.bfloat16)
    work = [pltpu.VMEM((2, SPAN, TX), jnp.float32), pltpu.VMEM((2, FRAME, TX), jnp.float32)]
    frames = shape((RANKS, FRAME, TX), jnp.bfloat16)

    one, two = call(
        rims_kernel,
        out_shape=(pltpu.VMEM(rim.shape, rim.dtype),) * 2,
        in_specs=[HBM] * 5,
        out_specs=(VMEM, VMEM),
        scratch_shapes=[
            pltpu.VMEM((2 * RIM + 1, TY, TX), jnp.bfloat16),
            pltpu.SMEM(offsets.shape, jnp.int32),
            pltpu.SMEM(fracs.shape, jnp.int32),
            pltpu.VMEM(rows.shape, jnp.float32),
            pltpu.VMEM(cols.shape, jnp.float32),
            *work,
            pltpu.SemaphoreType.DMA((6,)),
        ],
        compiler_params=wide,
        cost_estimate=cost(10**6, 10**6),
        name="rims",
    )(tiles, offsets, fracs, rows, cols)
    got_one, got_two = exchange(one, 0), exchange(two, 1)
    own, own_rim = call(
        own_kernel,
        out_shape=(frames, shape((2 * RIM, FRAME, TX), jnp.float32)),
        in_specs=[VMEM, SMEM, SMEM, VMEM, VMEM],
        out_specs=(ANY, VMEM),
        scratch_shapes=[
            *work,
            pltpu.VMEM((GROUPZ - 2 * RIM, FRAME, TX), jnp.bfloat16),
            pltpu.SemaphoreType.DMA((GROUPZ - 2 * RIM,)),
        ],
        compiler_params=params,
        cost_estimate=cost(10**7, 3 * 10**6),
        name="own",
    )(tiles, offsets, fracs, rows, cols)
    merged = call(
        merge_kernel,
        out_shape=frames,
        in_specs=[ANY, VMEM, VMEM, VMEM],
        out_specs=ANY,
        scratch_shapes=[pltpu.VMEM((2 * RIM, FRAME, TX), jnp.bfloat16), pltpu.SemaphoreType.DMA((2,))],
        input_output_aliases={0: 0},
        compiler_params=params,
        cost_estimate=cost(3 * 10**6, 2 * 10**6),
        name="merge",
    )(own, own_rim, got_one, got_two)
    received = lax.all_to_all(merged, "tile", split_axis=0, concat_axis=0, tiled=True)
    recip = call(
        weights_kernel,
        out_shape=shape((MYP, TX), jnp.float32),
        in_specs=[SMEM, VMEM, VMEM],
        out_specs=VMEM,
        compiler_params=params,
        cost_estimate=cost(10**7, 4 * 10**6),
        name="weights",
    )(offsets, rows, cols)
    return call(
        join_kernel,
        out_shape=shape((1, MY, TX), jnp.bfloat16),
        in_specs=[VMEM, VMEM],
        out_specs=VMEM,
        scratch_shapes=[pltpu.VMEM((MYP, TX), jnp.float32)],
        compiler_params=params,
        cost_estimate=cost(10**6, 4 * 10**6),
        name="join",
    )(received, recip)


def solution(mesh):
    in_specs = (P(("slab", "tile"), None, None, None), P(), P())
    out_specs = P(("slab", "tile"), None, None)
    return jax.shard_map(shards, mesh=mesh, in_specs=in_specs, out_specs=out_specs, check_vma=False)
```
